1024 devices in a mesh: dom: 16 (over x, z_lo), orb: 64 (over z_hi, y, core).
Axes of the slice: x: 8, y: 8, z: 8 (z_hi: 4, z_lo: 2; z = z_hi * 2 + z_lo), core: 2. Of those that a mesh axis runs over, the one named last changes fastest.
Arguments:
- orbitals: float32 [128, 256, 768], P('dom', 'orb'), may hold values from -24 to 24
- potential: float32 [128, 768], P('dom'), may hold values from -2 to 2
Outputs:
- gram_blocks: float32 [2, 256, 256], P(None, 'orb', 'dom')
The draws below stay inside these ranges and needn't reach their ends.
All inputs are finite; a program needn't handle non-finite values.
Results may differ from the reference program's by a relative error of at most 0.00005.
Values sent between devices are 32-bit elements; how exact they have to be, the bound alone decides.
A program may use at most 32 MiB of HBM per device.

```python
import jax
import jax.numpy as jnp
from jax import lax

NZ = 96
NY = 8
ORB_DEV = 4
DEGREE = 2
NX = 128
ORBS = 256
PLANE = 768
CELLS = 98304


def draw_orbitals(key, part):
    keys = jax.random.split(key, 3)
    noise = jax.random.truncated_normal(keys[0], -4.0, 4.0, (NX, ORBS, PLANE), jnp.float32)
    fields = jax.random.truncated_normal(keys[1], -4.0, 4.0, (NX, 8, PLANE), jnp.float32)
    mixing = jax.random.uniform(keys[2], (ORBS, 8), jnp.float32, -0.9, 0.9)
    envelope = 1.0 + 2.0 * jnp.arange(NX, dtype=jnp.float32) / max(NX - 1, 1)
    common = jnp.einsum('ok,xkp->xop', mixing, fields) * envelope[:, None, None]
    return jnp.clip(noise + common, -24.0, 24.0)


def steps_of(stream_key, dims, cuts, least, high):
    loudness = 1.0
    for axis_at, shards_of in cuts:
        heights = jax.random.uniform(jax.random.fold_in(jax.random.fold_in(stream_key, 6), axis_at), (shards_of,), jnp.float32, least / len(cuts), high / len(cuts))
        loudness = loudness * jnp.repeat(jnp.exp(heights), dims[axis_at] // shards_of).reshape((-1,) + (1,) * (len(dims) - 1 - axis_at))
    return loudness


def setup_inputs(seed: int = 0) -> dict:
    seeds = jax.random.split(jax.random.key(seed), 3)
    return {
        "orbitals": draw_orbitals(jax.random.fold_in(seeds[2], 71), 0),
        "potential": jnp.clip(jax.random.uniform(seeds[1], (NX, PLANE), jnp.float32, -2.0, 2.0) * steps_of(seeds[1], (NX, PLANE), ((0, 16),), -0.4, 0.0), -2.0, 2.0),
    }


coeffs = (-5369.0 / 1800.0, 12.0 / 7.0, -15.0 / 56.0, 10.0 / 189.0, -1.0 / 112.0, 2.0 / 1925.0, -1.0 / 16632.0)
center_value = 6.5
half_value = 6.5


def hamiltonian(field, potential):
    planes = field.shape[0]
    count = field.shape[1]
    cube = field.reshape(planes, count, NY, NZ)
    lap = 3.0 * coeffs[0] * cube
    for step in range(1, 7):
        near = jnp.roll(cube, step, 0) + jnp.roll(cube, -step, 0)
        near = near + jnp.roll(cube, step, 2) + jnp.roll(cube, -step, 2)
        near = near + jnp.roll(cube, step, 3) + jnp.roll(cube, -step, 3)
        lap = lap + coeffs[step] * near
    return (-0.5 * lap).reshape(planes, count, NY * NZ) + potential[:, None, :] * field


def reference(orbitals, potential):
    groups = ORBS // ORB_DEV
    blocks = orbitals.reshape(NX, groups, ORB_DEV, PLANE).transpose(1, 0, 2, 3)

    def filtering(block):
        previous = block
        current = (hamiltonian(block, potential) - center_value * block) / half_value
        for step in range(DEGREE - 1):
            following = 2.0 * (hamiltonian(current, potential) - center_value * current) / half_value - previous
            previous = current
            current = following
        return current, hamiltonian(current, potential)

    filtered, applied = lax.map(filtering, blocks)
    filtered = filtered.transpose(0, 2, 1, 3).reshape(ORBS, NX * PLANE)
    applied = applied.transpose(0, 2, 1, 3).reshape(ORBS, NX * PLANE)
    correlation = jnp.dot(filtered, filtered.T, precision=lax.Precision.HIGHEST, preferred_element_type=jnp.float32) / CELLS
    projected = jnp.dot(filtered, applied.T, precision=lax.Precision.HIGHEST, preferred_element_type=jnp.float32) / CELLS
    return jnp.stack([correlation, projected])
```

```python
import jax
import jax.numpy as jnp
from jax import lax
from jax.experimental import pallas as pl
from jax.experimental.pallas import tpu as pltpu
from jax.sharding import PartitionSpec as P

NZ = 96
NY = 8
CELLS = 98304
MESH = pl.DeviceIdType.MESH

coeffs = (
    -5369.0 / 1800.0,
    12.0 / 7.0,
    -15.0 / 56.0,
    10.0 / 189.0,
    -1.0 / 112.0,
    2.0 / 1925.0,
    -1.0 / 16632.0,
)
CENTER = 6.5
HALF = 6.5

LEFT = 12
EXT = 46
FIRST = 34
SECOND = 22
OWN = 16


def place(x, y, z, core):
    return {"dom": x * 2 + z % 2, "orb": (z // 2) * 16 + y * 2 + core}


def in_plane(tile, scale):
    along_z = [pltpu.roll(tile, j, 1) + pltpu.roll(tile, 128 - j, 1) for j in range(1, 7)]
    turned = [None] + [pltpu.roll(tile, k, 0) for k in range(1, 8)]
    along_y = (scale * coeffs[1]) * (turned[1] + turned[7])
    along_y += (scale * (coeffs[2] + coeffs[6])) * (turned[2] + turned[6])
    along_y += (scale * (coeffs[3] + coeffs[5])) * (turned[3] + turned[5])
    along_y += (scale * 2.0 * coeffs[4]) * turned[4]
    return along_z, along_y


def wrap_lanes(tile, lane):
    tile = jnp.where(lane >= NZ, pltpu.roll(tile, NZ, 1), tile)
    return jnp.where(lane >= 112, pltpu.roll(tile, 32, 1), tile)


def kernel(
    orb_ref,
    pot_ref,
    out_ref,
    raw,
    raw_pot,
    field0,
    field1,
    field2,
    poten,
    send_y,
    recv_y,
    recv_zc,
    rows_f,
    rows_g,
    cols_f,
    cols_g,
    part,
    part_core,
    sums_y,
    part_y,
    sums_x,
    part_x,
    sums_z,
    part_z,
    halo_out,
    halo_in,
    y_out,
    y_in,
    zc_out,
    zc_in,
    core_out,
    core_in,
    ry_out,
    ry_in,
    rx_out,
    rx_in,
    rz_out,
    rz_in,
):
    dom = lax.axis_index("dom")
    orb = lax.axis_index("orb")
    x, zl = dom // 2, dom % 2
    core, y, zh = orb % 2, (orb // 2) % 8, orb // 16
    z = zh * 2 + zl
    zc = z * 2 + core
    right, left = (x + 1) % 8, (x + 7) % 8
    right2, left2 = (x + 2) % 8, (x + 6) % 8
    pair = z + 1 - 2 * zl
    z0 = zh * 2
    lane = lax.broadcasted_iota(jnp.int32, (8, 128), 1)

    barrier = pltpu.get_barrier_semaphore()

    def greet(device):
        pl.semaphore_signal(barrier, inc=1, device_id=device, device_id_type=MESH)

    for i in range(1, 8):
        greet(place(x, y ^ i, z, core))
        greet(place(x ^ i, y, z, core))
    for i in range(1, 16):
        other = zc ^ i
        greet(place(x, y, other // 2, other % 2))
    greet(place(right, y, pair, core))
    greet(place(left, y, pair, core))

    @pl.when(zl == 1)
    def _():
        greet(place(right2, y, pair, core))

    own_row = pl.multiple_of(24 + 16 * zl, 8)
    raw[pl.ds(own_row, 16), :] = orb_ref[zl]
    own_pot = pl.multiple_of(16 + 8 * zl, 8)
    raw_pot[pl.ds(own_pot, 8), :] = pot_ref[...]
    pl.semaphore_wait(barrier, 32 - zl)

    def orb_copy(half, start, count, row, slot, device):
        return pltpu.make_async_remote_copy(
            src_ref=orb_ref.at[half, pl.ds(start, count)],
            dst_ref=raw.at[pl.ds(row, count)],
            send_sem=halo_out.at[slot],
            recv_sem=halo_in.at[slot],
            device_id=device,
            device_id_type=MESH,
        )

    def pot_copy(row, slot, device, out_slot):
        return pltpu.make_async_remote_copy(
            src_ref=pot_ref,
            dst_ref=raw_pot.at[pl.ds(row, 8)],
            send_sem=halo_out.at[out_slot],
            recv_sem=halo_in.at[slot],
            device_id=device,
            device_id_type=MESH,
        )

    copies = [(orb_copy(1 - zl, 0, 16, own_row, 0, place(x, y, pair, core)), None)]
    pots = [(pot_copy(own_pot, 6, place(x, y, pair, core), 8), None)]
    for t in range(2):
        to_left = place(left, y, z0 + t, core)
        to_right = place(right, y, z0 + t, core)
        to_left2 = place(left2, y, z0 + t, core)
        for mine in range(2):
            row = 56 + 16 * mine
            slot = 1 + mine
            copies.append((to_left, t, mine, 0, 16, row, slot))
            pots.append((to_left, mine, 32 + 8 * mine, 7 + mine))
        copies.append((to_right, t, 0, 8, 8, 0, 4))
        copies.append((to_right, t, 1, 0, 16, 8, 5))
        pots.append((to_right, 1, 8, 9))
        copies.append((to_left2, t, 0, 0, 4, 88, 3))

    copies[0][0].start()
    pots[0][0].start()

    def guarded(mine, action):
        pl.when(zl == mine)(action)

    def outgoing(mine):
        result = []
        at = 1
        for device, t, who, start, count, row, slot in copies[1:]:
            if who == mine:
                result.append(
                    pltpu.make_async_remote_copy(
                        src_ref=orb_ref.at[t, pl.ds(start, count)],
                        dst_ref=raw.at[pl.ds(row, count)],
                        send_sem=halo_out.at[at],
                        recv_sem=halo_in.at[slot],
                        device_id=device,
                        device_id_type=MESH,
                    )
                )
                at += 1
        at = 9
        for device, who, row, slot in pots[1:]:
            if who == mine:
                result.append(pot_copy(row, slot, device, at))
                at += 1
        return result

    for mine in range(2):

        @pl.when(zl == mine)
        def _(mine=mine):
            for copy in outgoing(mine):
                copy.start()

    me = place(x, y, pair, core)
    orb_copy(0, 0, 16, pl.multiple_of(40 - 16 * zl, 8), 0, me).wait_recv()
    orb_copy(0, 0, 16, 56, 1, me).wait_recv()
    orb_copy(0, 0, 16, 72, 2, me).wait_recv()
    orb_copy(0, 0, 4, 88, 3, me).wait_recv()
    orb_copy(0, 8, 8, 0, 4, me).wait_recv()
    orb_copy(0, 0, 16, 8, 5, me).wait_recv()
    pot_copy(pl.multiple_of(24 - 8 * zl, 8), 6, me, 8).wait_recv()
    for slot, row in ((7, 32), (8, 40), (9, 8)):
        pot_copy(row, slot, me, 8).wait_recv()

    def spread(block, _):
        row = pl.multiple_of(block * 8, 8)
        for yy in range(NY):
            tile = raw[pl.ds(row, 8), NZ * yy : NZ * yy + NZ]
            tile = jnp.concatenate([tile, tile[:, :16], tile[:, NZ - 16 :]], axis=1)
            field0[pl.ds(row * 8 + yy, 8, stride=8), :] = tile
        return 0

    lax.fori_loop(0, 12, spread, 0)

    def spread_pot(block, _):
        row = pl.multiple_of(block * 8, 8)
        for yy in range(NY):
            tile = raw_pot[pl.ds(row, 8), NZ * yy : NZ * yy + NZ]
            tile = jnp.concatenate([tile, tile[:, :32]], axis=1)
            poten[pl.ds(row * 8 + yy, 8, stride=8), :] = tile
        return 0

    lax.fori_loop(1, 6, spread_pot, 0)

    def load(ref, plane, k):
        return ref[pl.ds(pl.multiple_of((plane * 2 + k) * 8, 8), 8), :]

    def shifted(ref, plane, k, scale, diagonal):
        tile = load(ref, plane, k)
        along_z, total = in_plane(tile, scale)
        for j in range(1, 7):
            near = along_z[j - 1] + (load(ref, plane + j, k) + load(ref, plane - j, k))
            total += (scale * coeffs[j]) * near
        return total + diagonal * tile, tile

    def potential(plane):
        return poten[pl.ds(pl.multiple_of((plane + 16) * 8, 8), 8), :]

    def first(step, _):
        for part_of in range(2):
            at = step * 2 + part_of
            diagonal = potential(at - 6) * (1.0 / HALF) + ((-1.5 * coeffs[0] - CENTER) / HALF)
            for k in range(2):
                total, _tile = shifted(field0, at + 6, k, -0.5 / HALF, diagonal)
                row = pl.multiple_of((at * 2 + k) * 8, 8)
                field1[pl.ds(row, 8), :] = wrap_lanes(total, lane)
        return 0

    lax.fori_loop(0, FIRST // 2, first, 0)

    def second(step, _):
        for part_of in range(2):
            at = step * 2 + part_of
            diagonal = potential(at) * (2.0 / HALF) + (2.0 * (-1.5 * coeffs[0] - CENTER) / HALF)
            for k in range(2):
                total, _tile = shifted(field1, at + 6, k, -1.0 / HALF, diagonal)
                total -= load(field0, at + LEFT, k)
                row = pl.multiple_of((at * 2 + k) * 8, 8)
                field2[pl.ds(row, 8), :] = wrap_lanes(total, lane)
        return 0

    lax.fori_loop(0, SECOND // 2, second, 0)

    rows_out = send_y.reshape(512, 128)

    def third(step, _):
        for part_of in range(2):
            at = step * 2 + part_of
            diagonal = potential(at) * 0.5 - 0.75 * coeffs[0]
            for k in range(2):
                tile = load(field2, at, k)
                along_z, total = in_plane(tile, -0.25)
                for j in range(1, 7):
                    near = along_z[j - 1] + 2.0 * load(field2, at + j, k)
                    total += (-0.25 * coeffs[j]) * near
                total += diagonal * tile
                rows_out[pl.ds(at * 4 + k, 8, stride=64), :] = jnp.where(lane < NZ, tile, 0.0)
                rows_out[pl.ds(at * 4 + 2 + k, 8, stride=64), :] = jnp.where(lane < NZ, total, 0.0)
        return 0

    lax.fori_loop(0, OWN // 2, third, 0)

    def y_copy(i):
        return pltpu.make_async_remote_copy(
            src_ref=send_y.at[y ^ i],
            dst_ref=recv_y.at[y],
            send_sem=y_out.at[i],
            recv_sem=y_in.at[i],
            device_id=place(x, y ^ i, z, core),
            device_id_type=MESH,
        )

    for i in range(1, 8):
        y_copy(i).start()
    recv_y[y] = send_y[y]
    for i in range(1, 8):
        y_copy(i).wait_recv()

    def zc_copy(i):
        other = zc ^ i
        return pltpu.make_async_remote_copy(
            src_ref=recv_y.at[:, other],
            dst_ref=recv_zc.at[pl.ds(zc * 8, 8)],
            send_sem=zc_out.at[i],
            recv_sem=zc_in.at[i],
            device_id=place(x, y, other // 2, other % 2),
            device_id_type=MESH,
        )

    for i in range(1, 16):
        zc_copy(i).start()
    recv_zc[pl.ds(zc * 8, 8)] = recv_y[:, zc]
    for i in range(1, 16):
        zc_copy(i).wait_recv()

    flat = recv_zc.reshape(512, 128)
    for zz in range(8):
        for k in range(2):
            for what, rows in ((0, rows_f), (2, rows_g)):
                rows[pl.ds(zz * 2 + k, 16, stride=16), :] = flat[
                    pl.ds(zz * 64 + what + k, 16, stride=4), :
                ]
            for cc in range(2):
                at = (zz // 2) * 64 + cc * 4 + (zz % 2) * 2 + k
                for what, cols in ((0, cols_f), (2, cols_g)):
                    cols[pl.ds(at, 8, stride=8), :] = flat[
                        pl.ds((zz * 2 + cc) * 32 + what + k, 8, stride=4), :
                    ]

    def product(a, b):
        return lax.dot_general(
            a,
            b,
            (((1,), (1,)), ((), ())),
            precision=lax.Precision.HIGHEST,
            preferred_element_type=jnp.float32,
        )

    part[:, 0:256] = product(rows_f[...], cols_f[...])
    part[:, 256:512] = product(rows_f[...], cols_g[...]) + product(rows_g[...], cols_f[...])

    def core_copy(i):
        block = y ^ i
        return pltpu.make_async_remote_copy(
            src_ref=part.at[pl.ds(pl.multiple_of((1 - core) * 128 + block * 16, 16), 16)],
            dst_ref=part_core.at[block],
            send_sem=core_out.at[i],
            recv_sem=core_in.at[i],
            device_id=place(x, y, z, 1 - core),
            device_id_type=MESH,
        )

    order = (1, 2, 3, 4, 5, 6, 7, 0)
    for i in order:
        core_copy(i).start()

    def ry_copy(i):
        return pltpu.make_async_remote_copy(
            src_ref=sums_y.at[y ^ i],
            dst_ref=part_y.at[y],
            send_sem=ry_out.at[i],
            recv_sem=ry_in.at[i],
            device_id=place(x, y ^ i, z, core),
            device_id_type=MESH,
        )

    for i in order:
        block = y ^ i
        core_copy(i).wait_recv()
        rows = pl.ds(pl.multiple_of(core * 128 + block * 16, 16), 16)
        sums_y[block] = part[rows, :] + part_core[block]
        if i:
            ry_copy(i).start()

    total = sums_y[y]
    for i in range(1, 8):
        ry_copy(i).wait_recv()
        total += part_y[y ^ i]

    for xx in range(8):
        c0, c1 = 32 * xx, 256 + 32 * xx
        sums_x[xx] = jnp.concatenate(
            [
                total[0:8, c0 : c0 + 32],
                total[8:16, c0 : c0 + 32],
                total[0:8, c1 : c1 + 32],
                total[8:16, c1 : c1 + 32],
            ],
            axis=1,
        )

    def rx_copy(i):
        return pltpu.make_async_remote_copy(
            src_ref=sums_x.at[x ^ i],
            dst_ref=part_x.at[x],
            send_sem=rx_out.at[i],
            recv_sem=rx_in.at[i],
            device_id=place(x ^ i, y, z, core),
            device_id_type=MESH,
        )

    for i in range(1, 8):
        rx_copy(i).start()
    tile = sums_x[x]
    for i in range(1, 8):
        rx_copy(i).wait_recv()
        tile += part_x[x ^ i]

    sums_z[...] = tile

    def rz_copy(i):
        return pltpu.make_async_remote_copy(
            src_ref=sums_z,
            dst_ref=part_z.at[z],
            send_sem=rz_out.at[i],
            recv_sem=rz_in.at[i],
            device_id=place(x, y, z ^ i, core),
            device_id_type=MESH,
        )

    for i in range(1, 8):
        rz_copy(i).start()
    for i in range(1, 8):
        rz_copy(i).wait_recv()
        tile += part_z[z ^ i]
    tile = pltpu.roll(tile, (128 - (zh // 2) * 32 - 16 * zl) % 128, 1)
    tile = pltpu.roll(tile, (zh % 2) * 4, 0) * (1.0 / CELLS)
    out_ref[0] = tile[0:4, 0:16]
    out_ref[1] = tile[0:4, 64:80]

    copies[0][0].wait_send()
    pots[0][0].wait_send()
    for mine in range(2):

        @pl.when(zl == mine)
        def _(mine=mine):
            for copy in outgoing(mine):
                copy.wait_send()

    for i in range(1, 8):
        y_copy(i).wait_send()
        ry_copy(i).wait_send()
        rx_copy(i).wait_send()
        rz_copy(i).wait_send()
    for i in range(1, 16):
        zc_copy(i).wait_send()
    for i in range(8):
        core_copy(i).wait_send()


def on_device(orbitals, potential):
    halves = orbitals.reshape(8, 2, 2, NY * NZ).transpose(1, 0, 2, 3).reshape(2, 16, NY * NZ)
    f32 = jnp.float32
    dma = pltpu.SemaphoreType.DMA
    vmem = pl.BlockSpec(memory_space=pltpu.VMEM)
    return pl.pallas_call(
        kernel,
        out_shape=jax.ShapeDtypeStruct((2, 4, 16), f32),
        in_specs=[vmem, vmem],
        out_specs=vmem,
        scratch_shapes=[
            pltpu.VMEM((96, NY * NZ), f32),
            pltpu.VMEM((48, NY * NZ), f32),
            pltpu.VMEM((96 * 8, 128), f32),
            pltpu.VMEM((FIRST * 16, 128), f32),
            pltpu.VMEM((SECOND * 16, 128), f32),
            pltpu.VMEM((48 * 8, 128), f32),
            pltpu.VMEM((8, 16, 4, 128), f32),
            pltpu.VMEM((8, 16, 4, 128), f32),
            pltpu.VMEM((128, 4, 128), f32),
            pltpu.VMEM((256, 128), f32),
            pltpu.VMEM((256, 128), f32),
            pltpu.VMEM((256, 128), f32),
            pltpu.VMEM((256, 128), f32),
            pltpu.VMEM((256, 512), f32),
            pltpu.VMEM((8, 16, 512), f32),
            pltpu.VMEM((8, 16, 512), f32),
            pltpu.VMEM((8, 16, 512), f32),
            pltpu.VMEM((8, 8, 128), f32),
            pltpu.VMEM((8, 8, 128), f32),
            pltpu.VMEM((8, 128), f32),
            pltpu.VMEM((8, 8, 128), f32),
            dma((16,)),
            dma((10,)),
            dma((8,)),
            dma((8,)),
            dma((16,)),
            dma((16,)),
            dma((8,)),
            dma((8,)),
            dma((8,)),
            dma((8,)),
            dma((8,)),
            dma((8,)),
            dma((8,)),
            dma((8,)),
        ],
        compiler_params=pltpu.CompilerParams(
            collective_id=0, has_side_effects=True, vmem_limit_bytes=32 * 1024 * 1024
        ),
        cost_estimate=pl.CostEstimate(
            flops=200_000_000, bytes_accessed=1_000_000, transcendentals=0
        ),
    )(halves, potential)


def solution(mesh):
    return jax.shard_map(
        on_device,
        mesh=mesh,
        in_specs=(P("dom", "orb", None), P("dom", None)),
        out_specs=P(None, "orb", "dom"),
        check_vma=False,
    )
```

```python
import jax
import jax.numpy as jnp
from jax import lax
from jax.experimental import pallas as pl
from jax.experimental.pallas import tpu as pltpu
from jax.sharding import PartitionSpec as P

NZ = 96
NY = 8
CELLS = 98304
MESH = pl.DeviceIdType.MESH

coeffs = (
    -5369.0 / 1800.0,
    12.0 / 7.0,
    -15.0 / 56.0,
    10.0 / 189.0,
    -1.0 / 112.0,
    2.0 / 1925.0,
    -1.0 / 16632.0,
)
CENTER = 6.5
HALF = 6.5


def place(x, y, z, core):
    return {"dom": x * 2 + z % 2, "orb": (z // 2) * 16 + y * 2 + core}


def distance(shape, axis):
    return lax.broadcasted_iota(jnp.int32, shape, axis)


def band_x(rows, columns, offset, both):
    gap = distance((rows, columns), 1) - distance((rows, columns), 0) - offset
    band = jnp.zeros((rows, columns), jnp.float32)
    for j in range(1, 7):
        if both:
            band = jnp.where((gap == 2 * j) | (gap == -2 * j), coeffs[j], band)
        else:
            band = jnp.where(gap == 2 * j, 2.0 * coeffs[j], band)
    return band


def band_z():
    rows, columns = distance((128, 128), 0), distance((128, 128), 1)
    gap = rows - columns
    inside = (rows < NZ) & (columns < NZ)
    band = jnp.zeros((128, 128), jnp.float32)
    for j in range(1, 7):
        near = (gap == j) | (gap == -j) | (gap == NZ - j) | (gap == j - NZ)
        band = jnp.where(near & inside, coeffs[j], band)
    return band


def dot(a, b):
    return lax.dot_general(
        a,
        b,
        (((1,), (0,)), ((), ())),
        precision=lax.Precision.HIGHEST,
        preferred_element_type=jnp.float32,
    )


def dot_t(a, b):
    return lax.dot_general(
        a,
        b,
        (((1,), (1,)), ((), ())),
        precision=lax.Precision.HIGHEST,
        preferred_element_type=jnp.float32,
    )


def kernel(
    orb_ref,
    pot_ref,
    out_ref,
    raw,
    raw_pot,
    field0,
    field1,
    field2,
    poten,
    x_one,
    x_two,
    x_three,
    z_all,
    sum_x,
    sum_z,
    send_f,
    send_g,
    mid_f,
    mid_g,
    last_f,
    last_g,
    rows_f,
    rows_g,
    cols_f,
    cols_g,
    corr,
    proj,
    corr_core,
    proj_core,
    corr_one,
    proj_one,
    corr_got,
    proj_got,
    corr_two,
    proj_two,
    corr_have,
    proj_have,
    sums_z,
    part_z,
    halo_out,
    halo_in,
    own_in,
    f_out,
    f_in,
    g_out,
    g_in,
    f2_out,
    f2_in,
    g2_out,
    g2_in,
    ca_out,
    ca_in,
    cb_out,
    cb_in,
    ra_out,
    ra_in,
    rb_out,
    rb_in,
    sa_out,
    sa_in,
    sb_out,
    sb_in,
    rz_out,
    rz_in,
):
    dom = lax.axis_index("dom")
    orb = lax.axis_index("orb")
    x, zl = dom // 2, dom % 2
    core, y, zh = orb % 2, (orb // 2) % 8, orb // 16
    z = zh * 2 + zl
    zc = z * 2 + core
    right, left = (x + 1) % 8, (x + 7) % 8
    right2, left2 = (x + 2) % 8, (x + 6) % 8
    pair = z + 1 - 2 * zl
    z0 = zh * 2

    raw[pl.ds(92, 4), :] = jnp.zeros((4, NY * NZ), jnp.float32)
    barrier = pltpu.get_barrier_semaphore()

    def greet(device):
        pl.semaphore_signal(barrier, inc=1, device_id=device, device_id_type=MESH)

    for i in range(1, 8):
        greet(place(x, y ^ i, z, core))
        greet(place(x ^ i, y, z, core))
    for i in range(1, 16):
        other = zc ^ i
        greet(place(x, y, other // 2, other % 2))
    greet(place(right, y, pair, core))
    greet(place(left, y, pair, core))

    @pl.when(zl == 1)
    def _():
        greet(place(right2, y, pair, core))

    own_row = pl.multiple_of(24 + 16 * zl, 8)
    raw[pl.ds(own_row, 16), :] = orb_ref[zl]
    own_pot = pl.multiple_of(16 + 8 * zl, 8)
    raw_pot[pl.ds(own_pot, 8), :] = pot_ref[...]

    x_one[...] = band_x(72, 96, 8, True)
    x_two[...] = band_x(48, 72, 16, True)
    x_three[...] = band_x(32, 48, 0, False)
    z_all[...] = band_z()

    def spread(start, blocks):
        def step(block, _):
            row = pl.multiple_of(start + block * 8, 8)
            for yy in range(NY):
                tile = raw[pl.ds(row, 8), NZ * yy : NZ * yy + NZ]
                tile = jnp.concatenate([tile, jnp.zeros((8, 32), jnp.float32)], axis=1)
                field0[pl.ds(row, 8), 128 * yy : 128 * yy + 128] = tile
            return 0

        lax.fori_loop(0, blocks, step, 0)

    def spread_pot(row):
        for yy in range(NY):
            tile = raw_pot[pl.ds(row, 8), NZ * yy : NZ * yy + NZ]
            tile = jnp.concatenate([tile, jnp.zeros((8, 32), jnp.float32)], axis=1)
            for k in range(2):
                poten[yy, pl.ds(row * 2 + k, 8, stride=2), :] = tile

    spread(own_row, 2)
    spread_pot(own_pot)
    pl.semaphore_wait(barrier, 32 - zl)

    def orb_copy(half, start, count, row, slot, device):
        return pltpu.make_async_remote_copy(
            src_ref=orb_ref.at[half, pl.ds(start, count)],
            dst_ref=raw.at[pl.ds(row, count)],
            send_sem=halo_out.at[slot],
            recv_sem=halo_in.at[slot],
            device_id=device,
            device_id_type=MESH,
        )

    def pot_copy(row, slot, device, out_slot):
        return pltpu.make_async_remote_copy(
            src_ref=pot_ref,
            dst_ref=raw_pot.at[pl.ds(row, 8)],
            send_sem=halo_out.at[out_slot],
            recv_sem=halo_in.at[slot],
            device_id=device,
            device_id_type=MESH,
        )

    copies = [(orb_copy(1 - zl, 0, 16, own_row, 0, place(x, y, pair, core)), None)]
    pots = [(pot_copy(own_pot, 6, place(x, y, pair, core), 8), None)]
    for t in range(2):
        to_left = place(left, y, z0 + t, core)
        to_right = place(right, y, z0 + t, core)
        to_left2 = place(left2, y, z0 + t, core)
        for mine in range(2):
            row = 56 + 16 * mine
            slot = 1 + mine
            copies.append((to_left, t, mine, 0, 16, row, slot))
            pots.append((to_left, mine, 32 + 8 * mine, 7 + mine))
        copies.append((to_right, t, 0, 8, 8, 0, 4))
        copies.append((to_right, t, 1, 0, 16, 8, 5))
        pots.append((to_right, 1, 8, 9))
        copies.append((to_left2, t, 0, 0, 4, 88, 3))

    copies[0][0].start()
    pots[0][0].start()

    def guarded(mine, action):
        pl.when(zl == mine)(action)

    def outgoing(mine):
        result = []
        at = 1
        for device, t, who, start, count, row, slot in copies[1:]:
            if who == mine:
                result.append(
                    pltpu.make_async_remote_copy(
                        src_ref=orb_ref.at[t, pl.ds(start, count)],
                        dst_ref=raw.at[pl.ds(row, count)],
                        send_sem=halo_out.at[at],
                        recv_sem=halo_in.at[slot],
                        device_id=device,
                        device_id_type=MESH,
                    )
                )
                at += 1
        at = 9
        for device, who, row, slot in pots[1:]:
            if who == mine:
                result.append(pot_copy(row, slot, device, at))
                at += 1
        return result

    for mine in range(2):

        @pl.when(zl == mine)
        def _(mine=mine):
            for copy in outgoing(mine):
                copy.start()

    me = place(x, y, pair, core)
    pair_row = pl.multiple_of(40 - 16 * zl, 8)
    pair_pot = pl.multiple_of(24 - 8 * zl, 8)
    orb_copy(0, 0, 16, pair_row, 0, me).wait_recv()
    spread(pair_row, 2)
    orb_copy(0, 0, 16, 56, 1, me).wait_recv()
    orb_copy(0, 0, 16, 72, 2, me).wait_recv()
    spread(56, 4)
    orb_copy(0, 8, 8, 0, 4, me).wait_recv()
    orb_copy(0, 0, 16, 8, 5, me).wait_recv()
    spread(0, 3)
    orb_copy(0, 0, 4, 88, 3, me).wait_recv()
    spread(88, 1)
    pot_copy(pair_pot, 6, me, 8).wait_recv()
    spread_pot(pair_pot)
    for slot, row in ((7, 32), (8, 40), (9, 8)):
        pot_copy(row, slot, me, 8).wait_recv()
        spread_pot(row)

    def columns(yy):
        return slice(128 * (yy % NY), 128 * (yy % NY) + 128)

    def apply(field, start, count, band, pot_row, scale, diagonal, finish):
        rows = slice(start, start + count)
        sum_x[0:count, :] = dot(band[...], field[...])
        stacked = jnp.concatenate([field[rows, columns(yy)] for yy in range(NY)], axis=0)
        sum_z[0 : count * NY, :] = dot(stacked, z_all[...])
        for yy in range(NY):
            here = field[rows, columns(yy)]
            total = sum_x[0:count, columns(yy)] + sum_z[count * yy : count * yy + count, :]
            total += coeffs[1] * (field[rows, columns(yy + 1)] + field[rows, columns(yy + 7)])
            total += (coeffs[2] + coeffs[6]) * (
                field[rows, columns(yy + 2)] + field[rows, columns(yy + 6)]
            )
            total += (coeffs[3] + coeffs[5]) * (
                field[rows, columns(yy + 3)] + field[rows, columns(yy + 5)]
            )
            total += (2.0 * coeffs[4]) * field[rows, columns(yy + 4)]
            weight = poten[yy, pot_row : pot_row + count, :] * diagonal[0] + diagonal[1]
            finish(yy, scale * total + weight * here)

    level = -1.5 * coeffs[0]

    def first(yy, value):
        field1[:, columns(yy)] = value

    apply(
        field0, 8, 72, x_one, 16, -0.5 / HALF, (1.0 / HALF, (level - CENTER) / HALF), first
    )

    def second(yy, value):
        value -= field0[24:72, columns(yy)]
        field2[:, columns(yy)] = value
        send_f[yy] = value[0:32]

    apply(
        field1,
        16,
        48,
        x_two,
        32,
        -1.0 / HALF,
        (2.0 / HALF, 2.0 * (level - CENTER) / HALF),
        second,
    )

    def f_copy(i):
        return pltpu.make_async_remote_copy(
            src_ref=send_f.at[y ^ i],
            dst_ref=mid_f.at[y],
            send_sem=f_out.at[i],
            recv_sem=f_in.at[i],
            device_id=place(x, y ^ i, z, core),
            device_id_type=MESH,
        )

    for i in range(1, 8):
        f_copy(i).start()
    mid_f[y] = send_f[y]

    def third(yy, value):
        send_g[yy] = value

    apply(field2, 0, 32, x_three, 32, -0.25, (0.5, 0.5 * level), third)

    def plane_of(ref, index):
        return ref.at[:, pl.ds(index * 2, 2)]

    def g_copy(i):
        other = zc ^ i
        return pltpu.make_async_remote_copy(
            src_ref=plane_of(send_g, other),
            dst_ref=plane_of(mid_g, zc),
            send_sem=g_out.at[i],
            recv_sem=g_in.at[i],
            device_id=place(x, y, other // 2, other % 2),
            device_id_type=MESH,
        )

    for i in range(1, 16):
        g_copy(i).start()
    own_g = pltpu.make_async_copy(plane_of(send_g, zc), plane_of(mid_g, zc), own_in.at[0])
    own_g.start()

    def f2_copy(i):
        other = zc ^ i
        return pltpu.make_async_remote_copy(
            src_ref=plane_of(mid_f, other),
            dst_ref=plane_of(last_f, zc),
            send_sem=f2_out.at[i],
            recv_sem=f2_in.at[i],
            device_id=place(x, y, other // 2, other % 2),
            device_id_type=MESH,
        )

    def g2_copy(i):
        return pltpu.make_async_remote_copy(
            src_ref=mid_g.at[y ^ i],
            dst_ref=last_g.at[y],
            send_sem=g2_out.at[i],
            recv_sem=g2_in.at[i],
            device_id=place(x, y ^ i, z, core),
            device_id_type=MESH,
        )

    for i in range(1, 8):
        f_copy(i).wait_recv()
    for i in range(1, 16):
        f2_copy(i).start()
    own_f = pltpu.make_async_copy(plane_of(mid_f, zc), plane_of(last_f, zc), own_in.at[1])
    own_f.start()
    own_g.wait()
    for i in range(1, 16):
        g_copy(i).wait_recv()
    for i in range(1, 8):
        g2_copy(i).start()
    last_g[y] = mid_g[y]

    def reorder(last, rows, cols):
        flat = last.reshape(256, 128)
        for yy in range(8):
            for cc in range(2):
                for k in range(2):
                    rows[pl.ds((cc * 8 + yy) * 16 + k, 8, stride=2), :] = flat[
                        pl.ds(yy * 32 + cc * 2 + k, 8, stride=4), :
                    ]
        for zz in range(8):
            for cc in range(2):
                for k in range(2):
                    cols[pl.ds((zz // 2) * 64 + cc * 4 + (zz % 2) * 2 + k, 8, stride=8), :] = flat[
                        pl.ds(zz * 4 + cc * 2 + k, 8, stride=32), :
                    ]

    own_f.wait()
    for i in range(1, 16):
        f2_copy(i).wait_recv()
    reorder(last_f, rows_f, cols_f)
    corr[...] = dot_t(rows_f[...], cols_f[...])

    order = (1, 2, 3, 4, 5, 6, 7, 0)

    def ca_copy(i):
        block = y ^ i
        return pltpu.make_async_remote_copy(
            src_ref=corr.at[pl.ds(pl.multiple_of((1 - core) * 128 + block * 16, 16), 16)],
            dst_ref=corr_core.at[block],
            send_sem=ca_out.at[i],
            recv_sem=ca_in.at[i],
            device_id=place(x, y, z, 1 - core),
            device_id_type=MESH,
        )

    def cb_copy(i):
        block = x ^ i
        return pltpu.make_async_remote_copy(
            src_ref=proj.at[1 - core, pl.ds(pl.multiple_of(block * 32, 32), 32)],
            dst_ref=proj_core.at[block],
            send_sem=cb_out.at[i],
            recv_sem=cb_in.at[i],
            device_id=place(x, y, z, 1 - core),
            device_id_type=MESH,
        )

    def ra_copy(i):
        return pltpu.make_async_remote_copy(
            src_ref=corr_one.at[y ^ i],
            dst_ref=corr_got.at[y],
            send_sem=ra_out.at[i],
            recv_sem=ra_in.at[i],
            device_id=place(x, y ^ i, z, core),
            device_id_type=MESH,
        )

    def rb_copy(i):
        return pltpu.make_async_remote_copy(
            src_ref=proj_one.at[x ^ i],
            dst_ref=proj_got.at[x],
            send_sem=rb_out.at[i],
            recv_sem=rb_in.at[i],
            device_id=place(x ^ i, y, z, core),
            device_id_type=MESH,
        )

    for i in order:
        ca_copy(i).start()
    for i in range(1, 8):
        g2_copy(i).wait_recv()
    reorder(last_g, rows_g, cols_g)
    both = dot_t(cols_f[...], rows_g[...]) + dot_t(cols_g[...], rows_f[...])
    proj[0] = both[:, 0:128]
    proj[1] = both[:, 128:256]
    for i in order:
        cb_copy(i).start()
    for i in order:
        block = y ^ i
        ca_copy(i).wait_recv()
        rows = pl.ds(pl.multiple_of(core * 128 + block * 16, 16), 16)
        corr_one[block] = corr[rows, :] + corr_core[block]
        if i:
            ra_copy(i).start()
    for i in order:
        block = x ^ i
        cb_copy(i).wait_recv()
        rows = pl.ds(pl.multiple_of(block * 32, 32), 32)
        proj_one[block] = proj[core, rows, :] + proj_core[block]
        if i:
            rb_copy(i).start()

    def sa_copy(i):
        return pltpu.make_async_remote_copy(
            src_ref=corr_two.at[x ^ i],
            dst_ref=corr_have.at[x],
            send_sem=sa_out.at[i],
            recv_sem=sa_in.at[i],
            device_id=place(x ^ i, y, z, core),
            device_id_type=MESH,
        )

    def sb_copy(i):
        return pltpu.make_async_remote_copy(
            src_ref=proj_two.at[y ^ i],
            dst_ref=proj_have.at[y],
            send_sem=sb_out.at[i],
            recv_sem=sb_in.at[i],
            device_id=place(x, y ^ i, z, core),
            device_id_type=MESH,
        )

    blank = jnp.zeros((8, 64), jnp.float32)
    total = corr_one[y]
    for i in range(1, 8):
        ra_copy(i).wait_recv()
        total += corr_got[y ^ i]
    for xx in range(8):
        at = slice(32 * xx, 32 * xx + 32)
        corr_two[xx] = jnp.concatenate([total[0:8, at], total[8:16, at], blank], axis=1)
    for i in range(1, 8):
        sa_copy(i).start()
    total = proj_one[x]
    for i in range(1, 8):
        rb_copy(i).wait_recv()
        total += proj_got[x ^ i]
    for yy in range(8):
        at = slice(16 * yy, 16 * yy + 16)
        proj_two[yy] = jnp.concatenate(
            [total[8 * b : 8 * b + 8, at] for b in range(4)] + [blank], axis=1
        )
    for i in range(1, 8):
        sb_copy(i).start()
    one = corr_two[x]
    for i in range(1, 8):
        sa_copy(i).wait_recv()
        one += corr_have[x ^ i]
    two = proj_two[y]
    for i in range(1, 8):
        sb_copy(i).wait_recv()
        two += proj_have[y ^ i]
    tile = one + pltpu.roll(two, 64, 1)

    sums_z[...] = tile

    def rz_copy(i):
        return pltpu.make_async_remote_copy(
            src_ref=sums_z,
            dst_ref=part_z.at[z],
            send_sem=rz_out.at[i],
            recv_sem=rz_in.at[i],
            device_id=place(x, y, z ^ i, core),
            device_id_type=MESH,
        )

    for i in range(1, 8):
        rz_copy(i).start()
    for i in range(1, 8):
        rz_copy(i).wait_recv()
        tile += part_z[z ^ i]
    tile = tile * (1.0 / CELLS)
    one = pltpu.roll(tile, (128 - (zh // 2) * 32 - 16 * zl) % 128, 1)
    out_ref[0] = pltpu.roll(one, (zh % 2) * 4, 0)[0:4, 0:16]
    two = pltpu.roll(tile, 64 - 32 * zl - 4 * zh, 1).T
    out_ref[1] = jnp.concatenate([two[0:4, :], two[16:20, :]], axis=1)

    copies[0][0].wait_send()
    pots[0][0].wait_send()
    for mine in range(2):

        @pl.when(zl == mine)
        def _(mine=mine):
            for copy in outgoing(mine):
                copy.wait_send()

    for i in range(1, 8):
        for copy in (f_copy, g2_copy, ra_copy, rb_copy, sa_copy, sb_copy, rz_copy):
            copy(i).wait_send()
    for i in range(1, 16):
        g_copy(i).wait_send()
        f2_copy(i).wait_send()
    for i in range(8):
        ca_copy(i).wait_send()
        cb_copy(i).wait_send()


def on_device(orbitals, potential):
    halves = orbitals.reshape(8, 2, 2, NY * NZ).transpose(1, 0, 2, 3).reshape(2, 16, NY * NZ)
    f32 = jnp.float32
    vmem = pl.BlockSpec(memory_space=pltpu.VMEM)
    buffers = (
        [(96, 768), (48, 768), (96, 1024), (72, 1024), (48, 1024), (8, 96, 128)]
        + [(72, 96), (48, 72), (32, 48), (128, 128), (72, 1024), (576, 128)]
        + [(8, 32, 128)] * 6
        + [(256, 128)] * 4
        + [(256, 256), (2, 256, 128)]
        + [(8, 16, 256), (8, 32, 128)] * 3
        + [(8, 8, 128)] * 4
        + [(8, 128), (8, 8, 128)]
    )
    sems = [16, 10, 2] + [8, 8, 16, 16, 16, 16, 8, 8] + [8] * 14
    return pl.pallas_call(
        kernel,
        out_shape=jax.ShapeDtypeStruct((2, 4, 16), f32),
        in_specs=[vmem, vmem],
        out_specs=vmem,
        scratch_shapes=[pltpu.VMEM(shape, f32) for shape in buffers]
        + [pltpu.SemaphoreType.DMA((count,)) for count in sems],
        compiler_params=pltpu.CompilerParams(
            collective_id=0, has_side_effects=True, vmem_limit_bytes=32 * 1024 * 1024
        ),
        cost_estimate=pl.CostEstimate(
            flops=200_000_000, bytes_accessed=1_000_000, transcendentals=0
        ),
    )(halves, potential)


def solution(mesh):
    return jax.shard_map(
        on_device,
        mesh=mesh,
        in_specs=(P("dom", "orb", None), P("dom", None)),
        out_specs=P(None, "orb", "dom"),
        check_vma=False,
    )
```

```python
import jax
import jax.numpy as jnp
from jax import lax
from jax.experimental import pallas as pl
from jax.experimental.pallas import tpu as pltpu
from jax.sharding import PartitionSpec as P

NZ = 96
NY = 8
CELLS = 98304
MESH = pl.DeviceIdType.MESH

coeffs = (
    -5369.0 / 1800.0,
    12.0 / 7.0,
    -15.0 / 56.0,
    10.0 / 189.0,
    -1.0 / 112.0,
    2.0 / 1925.0,
    -1.0 / 16632.0,
)
CENTER = 6.5
HALF = 6.5

FAR = (4, 3, 5, 2, 6, 1, 7)
FAR_PAIRS = tuple(2 * d + flip for d in FAR for flip in range(2)) + (1,)


def place(x, y, z, core):
    return {"dom": x * 2 + z % 2, "orb": (z // 2) * 16 + y * 2 + core}


def distance(shape, axis):
    return lax.broadcasted_iota(jnp.int32, shape, axis)


def band_x(rows, columns, offset, both):
    gap = distance((rows, columns), 1) - distance((rows, columns), 0) - offset
    band = jnp.zeros((rows, columns), jnp.float32)
    for j in range(1, 7):
        if both:
            band = jnp.where((gap == 2 * j) | (gap == -2 * j), coeffs[j], band)
        else:
            band = jnp.where(gap == 2 * j, 2.0 * coeffs[j], band)
    return band


def band_z():
    rows, columns = distance((256, 256), 0), distance((256, 256), 1)
    gap = rows - columns
    same = (rows // 128 == columns // 128) & (rows % 128 < NZ) & (columns % 128 < NZ)
    band = jnp.zeros((256, 256), jnp.float32)
    for j in range(1, 7):
        near = (gap == j) | (gap == -j) | (gap == NZ - j) | (gap == j - NZ)
        band = jnp.where(near & same, coeffs[j], band)
    return band


def dot(a, b):
    return lax.dot_general(
        a,
        b,
        (((1,), (0,)), ((), ())),
        precision=lax.Precision.HIGHEST,
        preferred_element_type=jnp.float32,
    )


def dot_t(a, b):
    return lax.dot_general(
        a,
        b,
        (((1,), (1,)), ((), ())),
        precision=lax.Precision.HIGHEST,
        preferred_element_type=jnp.float32,
    )


def kernel(
    orb_hbm,
    pot_hbm,
    out_ref,
    orb_raw,
    orb_ref,
    pot_ref,
    raw,
    raw_pot,
    field0,
    field1,
    field2,
    poten,
    x_one,
    x_two,
    x_three,
    z_all,
    sum_x,
    sum_z,
    send_f,
    send_g,
    mid_f,
    mid_g,
    last_f,
    last_g,
    turn_f,
    turn_g,
    back_g,
    rows_f,
    rows_g,
    cols_f,
    cols_g,
    corr,
    proj,
    corr_core,
    proj_core,
    corr_one,
    proj_one,
    corr_got,
    proj_got,
    corr_two,
    proj_two,
    corr_have,
    proj_have,
    sums_z,
    part_z,
    halo_out,
    halo_in,
    own_in,
    f_out,
    f_in,
    g_out,
    g_in,
    f2_out,
    f2_in,
    g2_out,
    g2_in,
    ca_out,
    ca_in,
    cb_out,
    cb_in,
    ra_out,
    ra_in,
    rb_out,
    rb_in,
    sa_out,
    sa_in,
    sb_out,
    sb_in,
    rz_out,
    rz_in,
    near,
):
    dom = lax.axis_index("dom")
    orb = lax.axis_index("orb")
    x, zl = dom // 2, dom % 2
    core, y, zh = orb % 2, (orb // 2) % 8, orb // 16
    z = zh * 2 + zl
    zc = z * 2 + core
    right, left = (x + 1) % 8, (x + 7) % 8
    right2, left2 = (x + 2) % 8, (x + 6) % 8
    pair = z + 1 - 2 * zl
    z0 = zh * 2

    raw[pl.ds(92, 4), :] = jnp.zeros((4, NY * NZ), jnp.float32)
    load_orb = pltpu.make_async_copy(orb_hbm, orb_raw, own_in.at[2])
    load_pot = pltpu.make_async_copy(pot_hbm, pot_ref, own_in.at[3])
    load_orb.start()
    load_pot.start()
    barrier = pltpu.get_barrier_semaphore()

    def greet(device):
        pl.semaphore_signal(barrier, inc=1, device_id=device, device_id_type=MESH)

    steps = (
        lambda d: place((x + d) % 8, y, z, core),
        lambda d: place(x, (y + d) % 8, z, core),
        lambda d: place(x, y, (z + d) % 8, core),
    )
    greet(place(right2, y, z0, core))
    greet(place(right, y, pair, core))
    greet(place(left, y, pair, core))
    for step in steps:
        greet(step(1))
        greet(step(7))
    greet(place(x, y, z, 1 - core))

    def tell(turn):
        for axis, step in enumerate(steps):
            for side in range(2):
                pl.semaphore_signal(
                    near.at[axis, side, turn],
                    inc=1,
                    device_id=step(7 if side else 1),
                    device_id_type=MESH,
                )

    def hear(turn):
        for axis in range(3):
            for side in range(2):
                pl.semaphore_wait(near.at[axis, side, turn], 1)

    own_row = pl.multiple_of(24 + 16 * zl, 8)
    load_orb.wait()
    for p in range(8):
        four = orb_raw[p]
        orb_ref[0, 2 * p : 2 * p + 2, :] = four[0:2]
        orb_ref[1, 2 * p : 2 * p + 2, :] = four[2:4]
    load_pot.wait()
    raw[pl.ds(own_row, 16), :] = orb_ref[zl]
    own_pot = pl.multiple_of(16 + 8 * zl, 8)
    raw_pot[pl.ds(own_pot, 8), :] = pot_ref[...]

    x_one[...] = band_x(72, 96, 8, True)
    x_two[...] = band_x(48, 72, 16, True)
    x_three[...] = band_x(32, 48, 0, False)
    z_all[...] = band_z()

    def spread(start, blocks):
        def step(block, _):
            row = pl.multiple_of(start + block * 8, 8)
            for yy in range(NY):
                tile = raw[pl.ds(row, 8), NZ * yy : NZ * yy + NZ]
                tile = jnp.concatenate([tile, jnp.zeros((8, 32), jnp.float32)], axis=1)
                field0[pl.ds(row, 8), 128 * yy : 128 * yy + 128] = tile
            return 0

        lax.fori_loop(0, blocks, step, 0)

    def spread_pot(row):
        for yy in range(NY):
            tile = raw_pot[pl.ds(row, 8), NZ * yy : NZ * yy + NZ]
            tile = jnp.concatenate([tile, jnp.zeros((8, 32), jnp.float32)], axis=1)
            for k in range(2):
                poten[yy, pl.ds(row * 2 + k, 8, stride=2), :] = tile

    spread(own_row, 2)
    spread_pot(own_pot)
    pl.semaphore_wait(barrier, 11 - 2 * zl)

    def orb_copy(half, start, count, row, slot, device):
        return pltpu.make_async_remote_copy(
            src_ref=orb_ref.at[half, pl.ds(start, count)],
            dst_ref=raw.at[pl.ds(row, count)],
            send_sem=halo_out.at[slot],
            recv_sem=halo_in.at[slot],
            device_id=device,
            device_id_type=MESH,
        )

    def pot_copy(row, slot, device, out_slot):
        return pltpu.make_async_remote_copy(
            src_ref=pot_ref,
            dst_ref=raw_pot.at[pl.ds(row, 8)],
            send_sem=halo_out.at[out_slot],
            recv_sem=halo_in.at[slot],
            device_id=device,
            device_id_type=MESH,
        )

    copies = [(orb_copy(1 - zl, 0, 16, own_row, 0, place(x, y, pair, core)), None)]
    pots = [(pot_copy(own_pot, 6, place(x, y, pair, core), 8), None)]
    for t in range(2):
        to_left = place(left, y, z0 + t, core)
        to_right = place(right, y, z0 + t, core)
        to_left2 = place(left2, y, z0 + t, core)
        for mine in range(2):
            row = 56 + 16 * mine
            slot = 1 + mine
            copies.append((to_left, t, mine, 0, 16, row, slot))
            pots.append((to_left, mine, 32 + 8 * mine, 7 + mine))
        copies.append((to_right, t, 0, 8, 8, 0, 4))
        copies.append((to_right, t, 1, 0, 16, 8, 5))
        pots.append((to_right, 1, 8, 9))
        copies.append((to_left2, t, 0, 0, 4, 88, 3))

    copies[0][0].start()
    pots[0][0].start()

    def guarded(mine, action):
        pl.when(zl == mine)(action)

    def outgoing(mine):
        result = []
        at = 1
        for device, t, who, start, count, row, slot in copies[1:]:
            if who == mine:
                result.append(
                    pltpu.make_async_remote_copy(
                        src_ref=orb_ref.at[t, pl.ds(start, count)],
                        dst_ref=raw.at[pl.ds(row, count)],
                        send_sem=halo_out.at[at],
                        recv_sem=halo_in.at[slot],
                        device_id=device,
                        device_id_type=MESH,
                    )
                )
                at += 1
        at = 9
        for device, who, row, slot in pots[1:]:
            if who == mine:
                result.append(pot_copy(row, slot, device, at))
                at += 1
        return result

    for mine in range(2):

        @pl.when(zl == mine)
        def _(mine=mine):
            for copy in outgoing(mine):
                copy.start()

    tell(0)
    me = place(x, y, pair, core)
    pair_row = pl.multiple_of(40 - 16 * zl, 8)
    pair_pot = pl.multiple_of(24 - 8 * zl, 8)
    orb_copy(0, 0, 16, pair_row, 0, me).wait_recv()
    spread(pair_row, 2)
    hear(0)
    tell(1)
    orb_copy(0, 0, 16, 56, 1, me).wait_recv()
    orb_copy(0, 0, 16, 72, 2, me).wait_recv()
    spread(56, 4)
    hear(1)
    tell(2)
    orb_copy(0, 8, 8, 0, 4, me).wait_recv()
    orb_copy(0, 0, 16, 8, 5, me).wait_recv()
    spread(0, 3)
    hear(2)
    tell(3)
    orb_copy(0, 0, 4, 88, 3, me).wait_recv()
    spread(88, 1)
    pot_copy(pair_pot, 6, me, 8).wait_recv()
    spread_pot(pair_pot)
    for slot, row in ((7, 32), (8, 40), (9, 8)):
        pot_copy(row, slot, me, 8).wait_recv()
        spread_pot(row)

    hear(3)

    def columns(yy):
        return slice(128 * (yy % NY), 128 * (yy % NY) + 128)

    def apply(field, start, count, band, pot_row, scale, diagonal, finish):
        rows = slice(start, start + count)
        sum_x[0:count, :] = dot(band[...], field[...])
        stacked = jnp.concatenate([field[rows, 256 * q : 256 * q + 256] for q in range(4)], axis=0)
        sum_z[0 : count * 4, :] = dot(stacked, z_all[...])
        for yy in range(NY):
            here = field[rows, columns(yy)]
            q, half = yy // 2, columns(yy % 2)
            total = sum_x[0:count, columns(yy)] + sum_z[count * q : count * q + count, half]
            total += coeffs[1] * (field[rows, columns(yy + 1)] + field[rows, columns(yy + 7)])
            total += (coeffs[2] + coeffs[6]) * (
                field[rows, columns(yy + 2)] + field[rows, columns(yy + 6)]
            )
            total += (coeffs[3] + coeffs[5]) * (
                field[rows, columns(yy + 3)] + field[rows, columns(yy + 5)]
            )
            total += (2.0 * coeffs[4]) * field[rows, columns(yy + 4)]
            weight = poten[yy, pot_row : pot_row + count, :] * diagonal[0] + diagonal[1]
            finish(yy, scale * total + weight * here)

    level = -1.5 * coeffs[0]

    def first(yy, value):
        field1[:, columns(yy)] = value

    apply(
        field0, 8, 72, x_one, 16, -0.5 / HALF, (1.0 / HALF, (level - CENTER) / HALF), first
    )

    def second(yy, value):
        value -= field0[24:72, columns(yy)]
        field2[:, columns(yy)] = value
        send_f[yy] = value[0:32]

    apply(
        field1,
        16,
        48,
        x_two,
        32,
        -1.0 / HALF,
        (2.0 / HALF, 2.0 * (level - CENTER) / HALF),
        second,
    )

    def f_copy(i):
        return pltpu.make_async_remote_copy(
            src_ref=send_f.at[(y + i) % 8],
            dst_ref=mid_f.at[y],
            send_sem=f_out.at[i],
            recv_sem=f_in.at[i],
            device_id=place(x, (y + i) % 8, z, core),
            device_id_type=MESH,
        )

    for i in FAR:
        f_copy(i).start()
    mid_f[y] = send_f[y]

    def third(yy, value):
        send_g[yy] = value

    apply(field2, 0, 32, x_three, 32, -0.25, (0.5, 0.5 * level), third)

    def by_plane(source, target):
        source, target = source.reshape(256, 128), target.reshape(256, 128)
        for p in range(16):
            for k in range(2):
                target[pl.ds(p * 16 + k, 8, stride=2), :] = source[
                    pl.ds(p * 2 + k, 8, stride=32), :
                ]

    def by_row(source, target):
        source, target = source.reshape(256, 128), target.reshape(256, 128)
        for yy in range(8):
            for p in (0, 8):
                for k in range(2):
                    target[pl.ds(yy * 32 + p * 2 + k, 8, stride=2), :] = source[
                        pl.ds(p * 16 + yy * 2 + k, 8, stride=16), :
                    ]

    by_plane(send_g, turn_g)

    def g_copy(i):
        other = ((z + i // 2) % 8) * 2 + core + (i % 2) * (1 - 2 * core)
        return pltpu.make_async_remote_copy(
            src_ref=turn_g.at[other],
            dst_ref=mid_g.at[zc],
            send_sem=g_out.at[i],
            recv_sem=g_in.at[i],
            device_id=place(x, y, other // 2, other % 2),
            device_id_type=MESH,
        )

    for i in FAR_PAIRS:
        g_copy(i).start()
    mid_g[zc] = turn_g[zc]

    def f2_copy(i):
        other = ((z + i // 2) % 8) * 2 + core + (i % 2) * (1 - 2 * core)
        return pltpu.make_async_remote_copy(
            src_ref=turn_f.at[other],
            dst_ref=last_f.at[zc],
            send_sem=f2_out.at[i],
            recv_sem=f2_in.at[i],
            device_id=place(x, y, other // 2, other % 2),
            device_id_type=MESH,
        )

    def g2_copy(i):
        return pltpu.make_async_remote_copy(
            src_ref=back_g.at[(y + i) % 8],
            dst_ref=last_g.at[y],
            send_sem=g2_out.at[i],
            recv_sem=g2_in.at[i],
            device_id=place(x, (y + i) % 8, z, core),
            device_id_type=MESH,
        )

    for i in FAR[::-1]:
        f_copy(i).wait_recv()
    by_plane(mid_f, turn_f)
    for i in FAR_PAIRS:
        f2_copy(i).start()
    last_f[zc] = turn_f[zc]
    for i in range(1, 16):
        g_copy(i).wait_recv()
    by_row(mid_g, back_g)
    for i in FAR:
        g2_copy(i).start()
    last_g[y] = back_g[y]

    def reorder(last, rows, cols, along_z, along_c, along_y):
        flat = last.reshape(256, 128)
        for cc in range(2):
            for k in range(2):
                for yy in range(8):
                    rows[pl.ds((cc * 8 + yy) * 16 + k, 8, stride=2), :] = flat[
                        pl.ds(yy * along_y + cc * along_c + k, 8, stride=along_z), :
                    ]
                for zz in range(8):
                    at = (zz // 2) * 64 + cc * 4 + (zz % 2) * 2 + k
                    cols[pl.ds(at, 8, stride=8), :] = flat[
                        pl.ds(zz * along_z + cc * along_c + k, 8, stride=along_y), :
                    ]

    copies[0][0].wait_send()
    pots[0][0].wait_send()
    for mine in range(2):

        @pl.when(zl == mine)
        def _(mine=mine):
            for copy in outgoing(mine):
                copy.wait_send()

    for i in range(1, 8):
        f_copy(i).wait_send()
    for i in range(1, 16):
        g_copy(i).wait_send()
    for i in range(1, 16):
        f2_copy(i).wait_recv()
    reorder(last_f, rows_f, cols_f, 32, 16, 2)
    corr[...] = dot_t(rows_f[...], cols_f[...])

    order = FAR + (0,)

    def ca_copy(i):
        block = (y + i) % 8
        return pltpu.make_async_remote_copy(
            src_ref=corr.at[pl.ds(pl.multiple_of((1 - core) * 128 + block * 16, 16), 16)],
            dst_ref=corr_core.at[block],
            send_sem=ca_out.at[i],
            recv_sem=ca_in.at[i],
            device_id=place(x, y, z, 1 - core),
            device_id_type=MESH,
        )

    def cb_copy(i):
        block = (x + i) % 8
        return pltpu.make_async_remote_copy(
            src_ref=proj.at[1 - core, pl.ds(pl.multiple_of(block * 32, 32), 32)],
            dst_ref=proj_core.at[block],
            send_sem=cb_out.at[i],
            recv_sem=cb_in.at[i],
            device_id=place(x, y, z, 1 - core),
            device_id_type=MESH,
        )

    def ra_copy(i):
        return pltpu.make_async_remote_copy(
            src_ref=corr_one.at[(y + i) % 8],
            dst_ref=corr_got.at[y],
            send_sem=ra_out.at[i],
            recv_sem=ra_in.at[i],
            device_id=place(x, (y + i) % 8, z, core),
            device_id_type=MESH,
        )

    def rb_copy(i):
        return pltpu.make_async_remote_copy(
            src_ref=proj_one.at[(x + i) % 8],
            dst_ref=proj_got.at[x],
            send_sem=rb_out.at[i],
            recv_sem=rb_in.at[i],
            device_id=place((x + i) % 8, y, z, core),
            device_id_type=MESH,
        )

    for i in order:
        ca_copy(i).start()
    for i in FAR[::-1]:
        g2_copy(i).wait_recv()
    reorder(last_g, rows_g, cols_g, 4, 2, 32)
    both = dot_t(cols_f[...], rows_g[...]) + dot_t(cols_g[...], rows_f[...])
    proj[0] = both[:, 0:128]
    proj[1] = both[:, 128:256]
    for i in order:
        cb_copy(i).start()
    for i in order:
        block = (y + i) % 8
        ca_copy(i).wait_recv()
        rows = pl.ds(pl.multiple_of(core * 128 + block * 16, 16), 16)
        corr_one[block] = corr[rows, :] + corr_core[block]
        if i:
            ra_copy(i).start()
    for i in order:
        block = (x + i) % 8
        cb_copy(i).wait_recv()
        rows = pl.ds(pl.multiple_of(block * 32, 32), 32)
        proj_one[block] = proj[core, rows, :] + proj_core[block]
        if i:
            rb_copy(i).start()

    def sa_copy(i):
        return pltpu.make_async_remote_copy(
            src_ref=corr_two.at[(x + i) % 8],
            dst_ref=corr_have.at[x],
            send_sem=sa_out.at[i],
            recv_sem=sa_in.at[i],
            device_id=place((x + i) % 8, y, z, core),
            device_id_type=MESH,
        )

    def sb_copy(i):
        return pltpu.make_async_remote_copy(
            src_ref=proj_two.at[(y + i) % 8],
            dst_ref=proj_have.at[y],
            send_sem=sb_out.at[i],
            recv_sem=sb_in.at[i],
            device_id=place(x, (y + i) % 8, z, core),
            device_id_type=MESH,
        )

    for i in range(1, 8):
        g2_copy(i).wait_send()
    for i in range(1, 16):
        f2_copy(i).wait_send()
    blank = jnp.zeros((8, 64), jnp.float32)
    total = corr_one[y]
    for i in FAR[::-1]:
        ra_copy(i).wait_recv()
        total += corr_got[(y + 8 - i) % 8]
    for xx in range(8):
        at = slice(32 * xx, 32 * xx + 32)
        corr_two[xx] = jnp.concatenate([total[0:8, at], total[8:16, at], blank], axis=1)
    for i in FAR:
        sa_copy(i).start()
    total = proj_one[x]
    for i in FAR[::-1]:
        rb_copy(i).wait_recv()
        total += proj_got[(x + 8 - i) % 8]
    for yy in range(8):
        at = slice(16 * yy, 16 * yy + 16)
        proj_two[yy] = jnp.concatenate(
            [total[8 * b : 8 * b + 8, at] for b in range(4)] + [blank], axis=1
        )
    for i in FAR:
        sb_copy(i).start()
    for i in range(8):
        ca_copy(i).wait_send()
        cb_copy(i).wait_send()
    one = corr_two[x]
    for i in FAR[::-1]:
        sa_copy(i).wait_recv()
        one += corr_have[(x + 8 - i) % 8]
    two = proj_two[y]
    for i in FAR[::-1]:
        sb_copy(i).wait_recv()
        two += proj_have[(y + 8 - i) % 8]
    tile = one + pltpu.roll(two, 64, 1)

    sums_z[...] = tile

    def rz_copy(i):
        return pltpu.make_async_remote_copy(
            src_ref=sums_z,
            dst_ref=part_z.at[z],
            send_sem=rz_out.at[i],
            recv_sem=rz_in.at[i],
            device_id=place(x, y, (z + i) % 8, core),
            device_id_type=MESH,
        )

    for i in FAR:
        rz_copy(i).start()
    for i in range(1, 8):
        for copy in (ra_copy, rb_copy, sa_copy, sb_copy):
            copy(i).wait_send()
    for i in FAR[::-1]:
        rz_copy(i).wait_recv()
        tile += part_z[(z + 8 - i) % 8]
    tile = tile * (1.0 / CELLS)
    one = pltpu.roll(tile, (128 - (zh // 2) * 32 - 16 * zl) % 128, 1)
    out_ref[0] = pltpu.roll(one, (zh % 2) * 4, 0)[0:4, 0:16]
    two = pltpu.roll(tile, 64 - 32 * zl - 4 * zh, 1).T
    out_ref[1] = jnp.concatenate([two[0:4, :], two[16:20, :]], axis=1)

    for i in range(1, 8):
        rz_copy(i).wait_send()


def on_device(orbitals, potential):
    f32 = jnp.float32
    hbm = pl.BlockSpec(memory_space=pl.ANY)
    buffers = (
        [(8, 4, 768), (2, 16, 768), (8, 768)]
        + [(96, 768), (48, 768), (96, 1024), (72, 1024), (48, 1024), (8, 96, 128)]
        + [(72, 96), (48, 72), (32, 48), (256, 256), (72, 1024), (288, 256)]
        + [(8, 32, 128)] * 3
        + [(16, 16, 128)] * 2
        + [(8, 32, 128)]
        + [(16, 16, 128)] * 2
        + [(8, 32, 128)]
        + [(256, 128)] * 4
        + [(256, 256), (2, 256, 128)]
        + [(8, 16, 256), (8, 32, 128)] * 3
        + [(8, 8, 128)] * 4
        + [(8, 128), (8, 8, 128)]
    )
    sems = [16, 10, 4] + [8, 8, 16, 16, 16, 16, 8, 8] + [8] * 14
    return pl.pallas_call(
        kernel,
        out_shape=jax.ShapeDtypeStruct((2, 4, 16), f32),
        in_specs=[hbm, hbm],
        out_specs=pl.BlockSpec(memory_space=pltpu.VMEM),
        scratch_shapes=[pltpu.VMEM(shape, f32) for shape in buffers]
        + [pltpu.SemaphoreType.DMA((count,)) for count in sems]
        + [pltpu.SemaphoreType.REGULAR((3, 2, 4))],
        compiler_params=pltpu.CompilerParams(
            collective_id=0, has_side_effects=True, vmem_limit_bytes=60 * 1024 * 1024
        ),
        cost_estimate=pl.CostEstimate(
            flops=200_000_000, bytes_accessed=1_000_000, transcendentals=0
        ),
    )(orbitals, potential)


def solution(mesh):
    return jax.shard_map(
        on_device,
        mesh=mesh,
        in_specs=(P("dom", "orb", None), P("dom", None)),
        out_specs=P(None, "orb", "dom"),
        check_vma=False,
    )
```

```python
import jax
import jax.numpy as jnp
from jax import lax
from jax.experimental import pallas as pl
from jax.experimental.pallas import tpu as pltpu
from jax.sharding import PartitionSpec as P

NZ = 96
NY = 8
CELLS = 98304
MESH = pl.DeviceIdType.MESH

coeffs = (
    -5369.0 / 1800.0,
    12.0 / 7.0,
    -15.0 / 56.0,
    10.0 / 189.0,
    -1.0 / 112.0,
    2.0 / 1925.0,
    -1.0 / 16632.0,
)
CENTER = 6.5
HALF = 6.5


def place(x, y, z, core):
    return {"dom": x * 2 + z % 2, "orb": (z // 2) * 16 + y * 2 + core}


def distance(shape, axis):
    return lax.broadcasted_iota(jnp.int32, shape, axis)


def band_x(rows, columns, offset, both):
    gap = distance((rows, columns), 1) - distance((rows, columns), 0) - offset
    band = jnp.zeros((rows, columns), jnp.float32)
    for j in range(1, 7):
        if both:
            band = jnp.where((gap == 2 * j) | (gap == -2 * j), coeffs[j], band)
        else:
            band = jnp.where(gap == 2 * j, 2.0 * coeffs[j], band)
    return band


def band_z():
    rows, columns = distance((128, 128), 0), distance((128, 128), 1)
    gap = rows - columns
    inside = (rows < NZ) & (columns < NZ)
    band = jnp.zeros((128, 128), jnp.float32)
    for j in range(1, 7):
        near = (gap == j) | (gap == -j) | (gap == NZ - j) | (gap == j - NZ)
        band = jnp.where(near & inside, coeffs[j], band)
    return band


def dot(a, b):
    return lax.dot_general(
        a,
        b,
        (((1,), (0,)), ((), ())),
        precision=lax.Precision.HIGHEST,
        preferred_element_type=jnp.float32,
    )


def dot_t(a, b):
    return lax.dot_general(
        a,
        b,
        (((1,), (1,)), ((), ())),
        precision=lax.Precision.HIGH,
        preferred_element_type=jnp.float32,
    )


def kernel(
    orb_ref,
    pot_ref,
    out_ref,
    raw,
    raw_pot,
    field0,
    field1,
    field2,
    poten,
    x_one,
    x_two,
    x_three,
    z_all,
    sum_x,
    sum_z,
    send_f,
    send_g,
    mid_f,
    mid_g,
    last_f,
    last_g,
    rows_f,
    rows_g,
    cols_f,
    cols_g,
    corr,
    proj,
    corr_core,
    proj_core,
    corr_one,
    proj_one,
    corr_got,
    proj_got,
    corr_two,
    proj_two,
    corr_have,
    proj_have,
    sums_z,
    part_z,
    halo_out,
    halo_in,
    own_in,
    f_out,
    f_in,
    g_out,
    g_in,
    f2_out,
    f2_in,
    g2_out,
    g2_in,
    ca_out,
    ca_in,
    cb_out,
    cb_in,
    ra_out,
    ra_in,
    rb_out,
    rb_in,
    sa_out,
    sa_in,
    sb_out,
    sb_in,
    rz_out,
    rz_in,
):
    dom = lax.axis_index("dom")
    orb = lax.axis_index("orb")
    x, zl = dom // 2, dom % 2
    core, y, zh = orb % 2, (orb // 2) % 8, orb // 16
    z = zh * 2 + zl
    zc = z * 2 + core
    right, left = (x + 1) % 8, (x + 7) % 8
    right2, left2 = (x + 2) % 8, (x + 6) % 8
    pair = z + 1 - 2 * zl
    z0 = zh * 2

    raw[pl.ds(92, 4), :] = jnp.zeros((4, NY * NZ), jnp.float32)
    barrier = pltpu.get_barrier_semaphore()

    def greet(device):
        pl.semaphore_signal(barrier, inc=1, device_id=device, device_id_type=MESH)

    for i in range(1, 8):
        greet(place(x, y ^ i, z, core))
        greet(place(x ^ i, y, z, core))
    for i in range(1, 16):
        other = zc ^ i
        greet(place(x, y, other // 2, other % 2))
    greet(place(right, y, pair, core))
    greet(place(left, y, pair, core))

    @pl.when(zl == 1)
    def _():
        greet(place(right2, y, pair, core))

    own_row = pl.multiple_of(24 + 16 * zl, 8)
    raw[pl.ds(own_row, 16), :] = orb_ref[zl]
    own_pot = pl.multiple_of(16 + 8 * zl, 8)
    raw_pot[pl.ds(own_pot, 8), :] = pot_ref[...]

    x_one[...] = band_x(72, 96, 8, True)
    x_two[...] = band_x(48, 72, 16, True)
    x_three[...] = band_x(32, 48, 0, False)
    z_all[...] = band_z()

    def spread(start, blocks):
        def step(block, _):
            row = pl.multiple_of(start + block * 8, 8)
            for yy in range(NY):
                tile = raw[pl.ds(row, 8), NZ * yy : NZ * yy + NZ]
                tile = jnp.concatenate([tile, jnp.zeros((8, 32), jnp.float32)], axis=1)
                field0[pl.ds(row, 8), 128 * yy : 128 * yy + 128] = tile
            return 0

        lax.fori_loop(0, blocks, step, 0)

    def spread_pot(row):
        for yy in range(NY):
            tile = raw_pot[pl.ds(row, 8), NZ * yy : NZ * yy + NZ]
            tile = jnp.concatenate([tile, jnp.zeros((8, 32), jnp.float32)], axis=1)
            for k in range(2):
                poten[yy, pl.ds(row * 2 + k, 8, stride=2), :] = tile

    spread(own_row, 2)
    spread_pot(own_pot)
    pl.semaphore_wait(barrier, 32 - zl)

    def orb_copy(half, start, count, row, slot, device):
        return pltpu.make_async_remote_copy(
            src_ref=orb_ref.at[half, pl.ds(start, count)],
            dst_ref=raw.at[pl.ds(row, count)],
            send_sem=halo_out.at[slot],
            recv_sem=halo_in.at[slot],
            device_id=device,
            device_id_type=MESH,
        )

    def pot_copy(row, slot, device, out_slot):
        return pltpu.make_async_remote_copy(
            src_ref=pot_ref,
            dst_ref=raw_pot.at[pl.ds(row, 8)],
            send_sem=halo_out.at[out_slot],
            recv_sem=halo_in.at[slot],
            device_id=device,
            device_id_type=MESH,
        )

    copies = [(orb_copy(1 - zl, 0, 16, own_row, 0, place(x, y, pair, core)), None)]
    pots = [(pot_copy(own_pot, 6, place(x, y, pair, core), 8), None)]
    for t in range(2):
        to_left = place(left, y, z0 + t, core)
        to_right = place(right, y, z0 + t, core)
        to_left2 = place(left2, y, z0 + t, core)
        for mine in range(2):
            row = 56 + 16 * mine
            slot = 1 + mine
            copies.append((to_left, t, mine, 0, 16, row, slot))
            pots.append((to_left, mine, 32 + 8 * mine, 7 + mine))
        copies.append((to_right, t, 0, 8, 8, 0, 4))
        copies.append((to_right, t, 1, 0, 16, 8, 5))
        pots.append((to_right, 1, 8, 9))
        copies.append((to_left2, t, 0, 0, 4, 88, 3))

    copies[0][0].start()
    pots[0][0].start()

    def guarded(mine, action):
        pl.when(zl == mine)(action)

    def outgoing(mine):
        result = []
        at = 1
        for device, t, who, start, count, row, slot in copies[1:]:
            if who == mine:
                result.append(
                    pltpu.make_async_remote_copy(
                        src_ref=orb_ref.at[t, pl.ds(start, count)],
                        dst_ref=raw.at[pl.ds(row, count)],
                        send_sem=halo_out.at[at],
                        recv_sem=halo_in.at[slot],
                        device_id=device,
                        device_id_type=MESH,
                    )
                )
                at += 1
        at = 9
        for device, who, row, slot in pots[1:]:
            if who == mine:
                result.append(pot_copy(row, slot, device, at))
                at += 1
        return result

    for mine in range(2):

        @pl.when(zl == mine)
        def _(mine=mine):
            for copy in outgoing(mine):
                copy.start()

    me = place(x, y, pair, core)
    pair_row = pl.multiple_of(40 - 16 * zl, 8)
    pair_pot = pl.multiple_of(24 - 8 * zl, 8)
    orb_copy(0, 0, 16, pair_row, 0, me).wait_recv()
    spread(pair_row, 2)
    orb_copy(0, 0, 16, 56, 1, me).wait_recv()
    orb_copy(0, 0, 16, 72, 2, me).wait_recv()
    spread(56, 4)
    orb_copy(0, 8, 8, 0, 4, me).wait_recv()
    orb_copy(0, 0, 16, 8, 5, me).wait_recv()
    spread(0, 3)
    orb_copy(0, 0, 4, 88, 3, me).wait_recv()
    spread(88, 1)
    pot_copy(pair_pot, 6, me, 8).wait_recv()
    spread_pot(pair_pot)
    for slot, row in ((7, 32), (8, 40), (9, 8)):
        pot_copy(row, slot, me, 8).wait_recv()
        spread_pot(row)

    def columns(yy):
        return slice(128 * (yy % NY), 128 * (yy % NY) + 128)

    def apply(field, start, count, band, pot_row, scale, diagonal, finish):
        rows = slice(start, start + count)
        sum_x[0:count, :] = dot(band[...], field[...])
        stacked = jnp.concatenate([field[rows, columns(yy)] for yy in range(NY)], axis=0)
        sum_z[0 : count * NY, :] = dot(stacked, z_all[...])
        for yy in range(NY):
            here = field[rows, columns(yy)]
            total = sum_x[0:count, columns(yy)] + sum_z[count * yy : count * yy + count, :]
            total += coeffs[1] * (field[rows, columns(yy + 1)] + field[rows, columns(yy + 7)])
            total += (coeffs[2] + coeffs[6]) * (
                field[rows, columns(yy + 2)] + field[rows, columns(yy + 6)]
            )
            total += (coeffs[3] + coeffs[5]) * (
                field[rows, columns(yy + 3)] + field[rows, columns(yy + 5)]
            )
            total += (2.0 * coeffs[4]) * field[rows, columns(yy + 4)]
            weight = poten[yy, pot_row : pot_row + count, :] * diagonal[0] + diagonal[1]
            finish(yy, scale * total + weight * here)

    level = -1.5 * coeffs[0]

    def first(yy, value):
        field1[:, columns(yy)] = value

    apply(
        field0, 8, 72, x_one, 16, -0.5 / HALF, (1.0 / HALF, (level - CENTER) / HALF), first
    )

    def second(yy, value):
        value -= field0[24:72, columns(yy)]
        field2[:, columns(yy)] = value
        send_f[yy] = value[0:32]

    apply(
        field1,
        16,
        48,
        x_two,
        32,
        -1.0 / HALF,
        (2.0 / HALF, 2.0 * (level - CENTER) / HALF),
        second,
    )

    def f_copy(i):
        return pltpu.make_async_remote_copy(
            src_ref=send_f.at[y ^ i],
            dst_ref=mid_f.at[y],
            send_sem=f_out.at[i],
            recv_sem=f_in.at[i],
            device_id=place(x, y ^ i, z, core),
            device_id_type=MESH,
        )

    for i in range(1, 8):
        f_copy(i).start()
    mid_f[y] = send_f[y]

    def third(yy, value):
        send_g[yy] = value

    apply(field2, 0, 32, x_three, 32, -0.25, (0.5, 0.5 * level), third)

    def plane_of(ref, index):
        return ref.at[:, pl.ds(index * 2, 2)]

    def g_copy(i):
        other = zc ^ i
        return pltpu.make_async_remote_copy(
            src_ref=plane_of(send_g, other),
            dst_ref=plane_of(mid_g, zc),
            send_sem=g_out.at[i],
            recv_sem=g_in.at[i],
            device_id=place(x, y, other // 2, other % 2),
            device_id_type=MESH,
        )

    for i in range(1, 16):
        g_copy(i).start()
    own_g = pltpu.make_async_copy(plane_of(send_g, zc), plane_of(mid_g, zc), own_in.at[0])
    own_g.start()

    def f2_copy(i):
        other = zc ^ i
        return pltpu.make_async_remote_copy(
            src_ref=plane_of(mid_f, other),
            dst_ref=plane_of(last_f, zc),
            send_sem=f2_out.at[i],
            recv_sem=f2_in.at[i],
            device_id=place(x, y, other // 2, other % 2),
            device_id_type=MESH,
        )

    def g2_copy(i):
        return pltpu.make_async_remote_copy(
            src_ref=mid_g.at[y ^ i],
            dst_ref=last_g.at[y],
            send_sem=g2_out.at[i],
            recv_sem=g2_in.at[i],
            device_id=place(x, y ^ i, z, core),
            device_id_type=MESH,
        )

    for i in range(1, 8):
        f_copy(i).wait_recv()
    for i in range(1, 16):
        f2_copy(i).start()
    own_f = pltpu.make_async_copy(plane_of(mid_f, zc), plane_of(last_f, zc), own_in.at[1])
    own_f.start()
    own_g.wait()
    for i in range(1, 16):
        g_copy(i).wait_recv()
    for i in range(1, 8):
        g2_copy(i).start()
    last_g[y] = mid_g[y]

    def reorder(last, rows, cols):
        flat = last.reshape(256, 128)
        for yy in range(8):
            for cc in range(2):
                for k in range(2):
                    rows[pl.ds((cc * 8 + yy) * 16 + k, 8, stride=2), :] = flat[
                        pl.ds(yy * 32 + cc * 2 + k, 8, stride=4), :
                    ]
        for zz in range(8):
            for cc in range(2):
                for k in range(2):
                    cols[pl.ds((zz // 2) * 64 + cc * 4 + (zz % 2) * 2 + k, 8, stride=8), :] = flat[
                        pl.ds(zz * 4 + cc * 2 + k, 8, stride=32), :
                    ]

    own_f.wait()
    for i in range(1, 16):
        f2_copy(i).wait_recv()
    reorder(last_f, rows_f, cols_f)
    corr[...] = dot_t(rows_f[...], cols_f[...])

    order = (1, 2, 3, 4, 5, 6, 7, 0)

    def ca_copy(i):
        block = y ^ i
        return pltpu.make_async_remote_copy(
            src_ref=corr.at[pl.ds(pl.multiple_of((1 - core) * 128 + block * 16, 16), 16)],
            dst_ref=corr_core.at[block],
            send_sem=ca_out.at[i],
            recv_sem=ca_in.at[i],
            device_id=place(x, y, z, 1 - core),
            device_id_type=MESH,
        )

    def cb_copy(i):
        block = x ^ i
        return pltpu.make_async_remote_copy(
            src_ref=proj.at[1 - core, pl.ds(pl.multiple_of(block * 32, 32), 32)],
            dst_ref=proj_core.at[block],
            send_sem=cb_out.at[i],
            recv_sem=cb_in.at[i],
            device_id=place(x, y, z, 1 - core),
            device_id_type=MESH,
        )

    def ra_copy(i):
        return pltpu.make_async_remote_copy(
            src_ref=corr_one.at[y ^ i],
            dst_ref=corr_got.at[y],
            send_sem=ra_out.at[i],
            recv_sem=ra_in.at[i],
            device_id=place(x, y ^ i, z, core),
            device_id_type=MESH,
        )

    def rb_copy(i):
        return pltpu.make_async_remote_copy(
            src_ref=proj_one.at[x ^ i],
            dst_ref=proj_got.at[x],
            send_sem=rb_out.at[i],
            recv_sem=rb_in.at[i],
            device_id=place(x ^ i, y, z, core),
            device_id_type=MESH,
        )

    for i in order:
        ca_copy(i).start()
    for i in range(1, 8):
        g2_copy(i).wait_recv()
    reorder(last_g, rows_g, cols_g)
    both = dot_t(cols_f[...], rows_g[...]) + dot_t(cols_g[...], rows_f[...])
    proj[0] = both[:, 0:128]
    proj[1] = both[:, 128:256]
    for i in order:
        cb_copy(i).start()
    for i in order:
        block = y ^ i
        ca_copy(i).wait_recv()
        rows = pl.ds(pl.multiple_of(core * 128 + block * 16, 16), 16)
        corr_one[block] = corr[rows, :] + corr_core[block]
        if i:
            ra_copy(i).start()
    for i in order:
        block = x ^ i
        cb_copy(i).wait_recv()
        rows = pl.ds(pl.multiple_of(block * 32, 32), 32)
        proj_one[block] = proj[core, rows, :] + proj_core[block]
        if i:
            rb_copy(i).start()

    def sa_copy(i):
        return pltpu.make_async_remote_copy(
            src_ref=corr_two.at[x ^ i],
            dst_ref=corr_have.at[x],
            send_sem=sa_out.at[i],
            recv_sem=sa_in.at[i],
            device_id=place(x ^ i, y, z, core),
            device_id_type=MESH,
        )

    def sb_copy(i):
        return pltpu.make_async_remote_copy(
            src_ref=proj_two.at[y ^ i],
            dst_ref=proj_have.at[y],
            send_sem=sb_out.at[i],
            recv_sem=sb_in.at[i],
            device_id=place(x, y ^ i, z, core),
            device_id_type=MESH,
        )

    blank = jnp.zeros((8, 64), jnp.float32)
    total = corr_one[y]
    for i in range(1, 8):
        ra_copy(i).wait_recv()
        total += corr_got[y ^ i]
    for xx in range(8):
        at = slice(32 * xx, 32 * xx + 32)
        corr_two[xx] = jnp.concatenate([total[0:8, at], total[8:16, at], blank], axis=1)
    for i in range(1, 8):
        sa_copy(i).start()
    total = proj_one[x]
    for i in range(1, 8):
        rb_copy(i).wait_recv()
        total += proj_got[x ^ i]
    for yy in range(8):
        at = slice(16 * yy, 16 * yy + 16)
        proj_two[yy] = jnp.concatenate(
            [total[8 * b : 8 * b + 8, at] for b in range(4)] + [blank], axis=1
        )
    for i in range(1, 8):
        sb_copy(i).start()
    one = corr_two[x]
    for i in range(1, 8):
        sa_copy(i).wait_recv()
        one += corr_have[x ^ i]
    two = proj_two[y]
    for i in range(1, 8):
        sb_copy(i).wait_recv()
        two += proj_have[y ^ i]
    tile = one + pltpu.roll(two, 64, 1)

    sums_z[...] = tile

    def rz_copy(i):
        return pltpu.make_async_remote_copy(
            src_ref=sums_z,
            dst_ref=part_z.at[z],
            send_sem=rz_out.at[i],
            recv_sem=rz_in.at[i],
            device_id=place(x, y, z ^ i, core),
            device_id_type=MESH,
        )

    for i in range(1, 8):
        rz_copy(i).start()
    for i in range(1, 8):
        rz_copy(i).wait_recv()
        tile += part_z[z ^ i]
    tile = tile * (1.0 / CELLS)
    one = pltpu.roll(tile, (128 - (zh // 2) * 32 - 16 * zl) % 128, 1)
    out_ref[0] = pltpu.roll(one, (zh % 2) * 4, 0)[0:4, 0:16]
    two = pltpu.roll(tile, 64 - 32 * zl - 4 * zh, 1).T
    out_ref[1] = jnp.concatenate([two[0:4, :], two[16:20, :]], axis=1)

    copies[0][0].wait_send()
    pots[0][0].wait_send()
    for mine in range(2):

        @pl.when(zl == mine)
        def _(mine=mine):
            for copy in outgoing(mine):
                copy.wait_send()

    for i in range(1, 8):
        for copy in (f_copy, g2_copy, ra_copy, rb_copy, sa_copy, sb_copy, rz_copy):
            copy(i).wait_send()
    for i in range(1, 16):
        g_copy(i).wait_send()
        f2_copy(i).wait_send()
    for i in range(8):
        ca_copy(i).wait_send()
        cb_copy(i).wait_send()


def on_device(orbitals, potential):
    halves = orbitals.reshape(8, 2, 2, NY * NZ).transpose(1, 0, 2, 3).reshape(2, 16, NY * NZ)
    f32 = jnp.float32
    vmem = pl.BlockSpec(memory_space=pltpu.VMEM)
    buffers = (
        [(96, 768), (48, 768), (96, 1024), (72, 1024), (48, 1024), (8, 96, 128)]
        + [(72, 96), (48, 72), (32, 48), (128, 128), (72, 1024), (576, 128)]
        + [(8, 32, 128)] * 6
        + [(256, 128)] * 4
        + [(256, 256), (2, 256, 128)]
        + [(8, 16, 256), (8, 32, 128)] * 3
        + [(8, 8, 128)] * 4
        + [(8, 128), (8, 8, 128)]
    )
    sems = [16, 10, 2] + [8, 8, 16, 16, 16, 16, 8, 8] + [8] * 14
    return pl.pallas_call(
        kernel,
        out_shape=jax.ShapeDtypeStruct((2, 4, 16), f32),
        in_specs=[vmem, vmem],
        out_specs=vmem,
        scratch_shapes=[pltpu.VMEM(shape, f32) for shape in buffers]
        + [pltpu.SemaphoreType.DMA((count,)) for count in sems],
        compiler_params=pltpu.CompilerParams(
            collective_id=0, has_side_effects=True, vmem_limit_bytes=32 * 1024 * 1024
        ),
        cost_estimate=pl.CostEstimate(
            flops=200_000_000, bytes_accessed=1_000_000, transcendentals=0
        ),
    )(halves, potential)


def solution(mesh):
    return jax.shard_map(
        on_device,
        mesh=mesh,
        in_specs=(P("dom", "orb", None), P("dom", None)),
        out_specs=P(None, "orb", "dom"),
        check_vma=False,
    )
```
